32 devices in a mesh: pack: 2 (over y), gx: 4 (over z), gy: 4 (over x, core).
Axes of the slice: x: 2, y: 2, z: 4, core: 2. Of those that a mesh axis runs over, the one named last changes fastest.
Arguments:
- modes_in: float32 [32, 3, 64, 512], P(None, None, ('pack', 'gx'), 'gy'), parts along dimension 2, may hold values from -6 to 6
- dirs_in: float32 [32, 3, 64, 512], P(None, None, ('pack', 'gx'), 'gy'), parts along dimension 2, may hold values from -6 to 6
- onsite: float32 [3, 64, 512], P(None, ('pack', 'gx'), 'gy'), parts along dimension 1, may hold values from 0.3 to 10
- bond_terms: float32 [8, 4, 64, 512], P(None, None, ('pack', 'gx'), 'gy'), parts along dimension 2, as said below
- contacts: int32 [8, 64, 512], P(None, ('pack', 'gx'), 'gy'), parts along dimension 1, may hold values from 0 to 1, as said below
Outputs:
- modes: float32 [32, 3, 64, 512], P(None, None, ('pack', 'gx'), 'gy'), parts along dimension 2
- ritz_values: float32 [64], P('pack'), parts along dimension 0
The draws below stay inside these ranges and needn't reach their ends.
There are 2 independent parts, one for each index of `pack`. The reference program is written for one: setup_inputs(seed, part) draws one part's arguments, and reference() takes and returns one part's arrays. A program takes and returns all parts, laid end to end along the dimension named above; each array names one. Nothing has to cross between parts.
Inputs may be any that keep to these rules, and one draw needn't show every extreme that they name: Contact lists are mutual: contacts[d + 4] at grain (x, y) equals contacts[d] at grain (x, y) - e_d, periodic, for d = 0..3 with e_0..e_3 = (1,0), (0,1), (1,1), (1,-1). bond_terms[d + 4] at grain (x, y) equals bond_terms[d] at grain (x, y) - e_d, periodic, for d = 0..3; bond_terms[d, 3] is positive.
All inputs are finite; a program needn't handle non-finite values.
Results may differ from the reference program's by a relative error of at most 0.0003.
Values sent between devices are 32-bit elements; how exact they have to be, the bound alone decides.
A program may use at most 64 MiB of HBM per device.

```python
import math
import jax
import jax.numpy as jnp
from jax import lax

MODES = 32
ITERS = 2
NX = 32
NY = 512


forward_offsets = ((1, 0), (0, 1), (1, 1), (1, -1))


def mirror_bonds(forward):
    backward = [jnp.roll(forward[d], (forward_offsets[d][0], forward_offsets[d][1]), axis=(-2, -1)) for d in range(4)]
    return jnp.concatenate([forward, jnp.stack(backward)], axis=0)


def draw_bond_terms(key, part):
    key = jax.random.fold_in(key, 11)
    key_vec, key_soft = jax.random.split(key)
    vectors = jnp.clip(jax.random.normal(key_vec, (4, 3, NX, NY), jnp.float32), -4.0, 4.0)
    stiffness = jnp.exp(jax.random.uniform(key_soft, (4, 1, NX, NY), jnp.float32, math.log(0.1), 0.0))
    forward = jnp.concatenate([vectors, stiffness], axis=1)
    return mirror_bonds(forward)


def draw_contacts(key, part):
    key = jax.random.fold_in(key, 23)
    forward = jax.random.randint(key, (4, NX, NY), 0, 2).astype(jnp.int32)
    return mirror_bonds(forward)


def block_levels(own_key, extent, cuts, low, top_value):
    level = 1.0
    for position, shards_of in cuts:
        draws = jax.random.uniform(jax.random.fold_in(jax.random.fold_in(own_key, 6), position), (shards_of,), jnp.float32, low / len(cuts), top_value / len(cuts))
        level = level * jnp.repeat(jnp.exp(draws), extent[position] // shards_of).reshape((-1,) + (1,) * (len(extent) - 1 - position))
    return level


def gaussian(stream_key, dims, width, limit, cuts=(), kind=jnp.bfloat16):
    gain = block_levels(stream_key, dims, cuts, -0.22, 0.18) if cuts else 1.0
    values = jax.random.normal(stream_key, dims, jnp.float32) * width * gain
    return jnp.minimum(jnp.maximum(values, -limit), limit).astype(kind)


def setup_inputs(seed: int = 0, part: int = 0) -> dict:
    key_list = jax.random.split(jax.random.key(seed), 6)
    part_splits = jax.random.split(jax.random.fold_in(key_list[5], part), 6)
    modes_in = gaussian(part_splits[0], (MODES, 3, NX, NY), 1.0, 6.0, ((2, 4), (3, 4)), jnp.float32)
    dirs_in = gaussian(part_splits[1], (MODES, 3, NX, NY), 1.0, 6.0, ((2, 4), (3, 4)), jnp.float32)
    onsite = jnp.clip(jnp.exp(math.log(10.0) - 3.506558 * jax.random.uniform(part_splits[2], (3, NX, NY), jnp.float32) ** block_levels(part_splits[2], (3, NX, NY), ((1, 4), (2, 4)), -0.2, 0.2)), 0.3, 10.0)
    bond_terms = draw_bond_terms(jax.random.fold_in(jax.random.fold_in(key_list[5], part), 71), part)
    contacts = draw_contacts(jax.random.fold_in(jax.random.fold_in(key_list[5], part), 71), part)
    return {"modes_in": modes_in, "dirs_in": dirs_in, "onsite": onsite, "bond_terms": bond_terms, "contacts": contacts}


highest = lax.Precision.HIGHEST
offsets = ((1, 0), (0, 1), (1, 1), (1, -1), (-1, 0), (0, -1), (-1, -1), (-1, 1))
third_turn = 2.0 * math.pi / 3.0

def bond_coefs(bond_terms, contacts):
    contact_on = contacts.astype(jnp.float32)
    bond_vecs = bond_terms[:, 0:3] * contact_on[:, None]
    bond_soft = bond_terms[:, 3] * contact_on
    return (bond_vecs, bond_soft)

def stretch_terms(result, field, beside, bond_vecs, bond_soft, direction):
    stretch = field - beside
    along = lax.optimization_barrier(jnp.sum(bond_vecs[direction][None] * stretch, axis=1, keepdims=True))
    return result + bond_vecs[direction][None] * along + bond_soft[direction][None, None] * stretch

def apply_hessian(field, bond_vecs, bond_soft, onsite):
    result = onsite[None] * field
    for direction in range(8):
        step_x, step_y = offsets[direction]
        beside = jnp.roll(field, (-step_x, -step_y), axis=(2, 3))
        result = stretch_terms(result, field, beside, bond_vecs, bond_soft, direction)
    return result

def diag_blocks(matrix, mode_count):
    return jnp.diagonal(matrix.reshape(3, mode_count, 3, mode_count), axis1=1, axis2=3)

def pencil_lowest(gram_diag, hess_diag):
    gram_sym = 0.5 * (gram_diag + jnp.swapaxes(gram_diag, 0, 1))
    hess_sym = 0.5 * (hess_diag + jnp.swapaxes(hess_diag, 0, 1))
    empty_entry = jnp.zeros_like(gram_sym[0, 0])
    factor = [[empty_entry for j in range(3)] for i in range(3)]
    for i in range(3):
        for j in range(i + 1):
            pivot = gram_sym[i, j] - sum((factor[i][k] * factor[j][k] for k in range(j)))
            if i == j:
                factor[i][i] = jnp.sqrt(pivot)
            else:
                factor[i][j] = pivot / factor[j][j]
    inverse = [[empty_entry for j in range(3)] for i in range(3)]
    for j in range(3):
        inverse[j][j] = 1.0 / factor[j][j]
        for i in range(j + 1, 3):
            inverse[i][j] = -sum((factor[i][k] * inverse[k][j] for k in range(j, i))) / factor[i][i]
    inv_lower = jnp.stack([jnp.stack(row) for row in inverse])
    reduced = jnp.einsum('ijm,jkm,lkm->ilm', inv_lower, hess_sym, inv_lower, precision=highest)
    middle = (reduced[0, 0] + reduced[1, 1] + reduced[2, 2]) / 3.0
    identity = jnp.eye(3, dtype=jnp.float32)[:, :, None]
    centred = reduced - middle[None, None] * identity
    spread = jnp.sqrt(lax.optimization_barrier(jnp.sum(centred * centred, axis=(0, 1))) / 6.0)
    determinant = centred[0, 0] * (centred[1, 1] * centred[2, 2] - centred[1, 2] * centred[2, 1]) - centred[0, 1] * (centred[1, 0] * centred[2, 2] - centred[1, 2] * centred[2, 0]) + centred[0, 2] * (centred[1, 0] * centred[2, 1] - centred[1, 1] * centred[2, 0])
    cosine = jnp.clip(determinant / (2.0 * spread * spread * spread), -1.0, 1.0)
    third_angle = jnp.arccos(cosine) / 3.0
    lowest = middle + 2.0 * spread * jnp.cos(third_angle + third_turn)
    pencil = hess_sym - lowest[None, None] * gram_sym
    vector = jnp.stack([pencil[1, 1] * pencil[2, 2] - pencil[1, 2] * pencil[2, 1], pencil[1, 2] * pencil[2, 0] - pencil[1, 0] * pencil[2, 2], pencil[1, 0] * pencil[2, 1] - pencil[1, 1] * pencil[2, 0]])
    return (lowest, vector)

def coefficients(vector, gram_diag):
    raw_coef = jnp.concatenate([jnp.diag(vector[0]), jnp.diag(vector[1]), jnp.diag(vector[2])], axis=0)
    dir_sq = vector[1] * vector[1] * gram_diag[1, 1] + vector[1] * vector[2] * (gram_diag[1, 2] + gram_diag[2, 1]) + vector[2] * vector[2] * gram_diag[2, 2]
    dir_scale = 1.0 / jnp.sqrt(dir_sq + 1e-06)
    dir_coef = jnp.concatenate([jnp.zeros_like(jnp.diag(vector[0])), jnp.diag(vector[1] * dir_scale), jnp.diag(vector[2] * dir_scale)], axis=0)
    return (raw_coef, dir_coef)

def reference(modes_in, dirs_in, onsite, bond_terms, contacts):
    bond_vecs, bond_soft = bond_coefs(bond_terms, contacts)
    mode_count = modes_in.shape[0]
    grid_shape = modes_in.shape
    entries = 3 * NX * NY
    current, search = (modes_in, dirs_in)
    mode_image = apply_hessian(current, bond_vecs, bond_soft, onsite)
    search_image = apply_hessian(search, bond_vecs, bond_soft, onsite)
    image_image = apply_hessian(mode_image, bond_vecs, bond_soft, onsite)
    lowest = jnp.zeros((mode_count,), jnp.float32)
    for sweep in range(ITERS):
        basis_rows = jnp.concatenate([current, mode_image, search], 0).reshape(3 * mode_count, -1)
        image_rows = jnp.concatenate([mode_image, image_image, search_image], 0).reshape(3 * mode_count, -1)
        gram = jnp.dot(basis_rows, basis_rows.T, precision=highest) / entries
        hess_gram = jnp.dot(basis_rows, image_rows.T, precision=highest) / entries
        gram_diag = diag_blocks(gram, mode_count)
        hess_diag = diag_blocks(hess_gram, mode_count)
        lowest, vector = pencil_lowest(gram_diag, hess_diag)
        raw_coef, dir_coef = coefficients(vector, gram_diag)
        mode_gram = jnp.dot(raw_coef.T, jnp.dot(gram, raw_coef, precision=highest), precision=highest)
        chol_lower = jnp.linalg.cholesky(mode_gram)
        raw_rows = jnp.dot(raw_coef.T, basis_rows, precision=highest)
        current = jax.scipy.linalg.solve_triangular(chol_lower, raw_rows, lower=True).reshape(grid_shape)
        search = jnp.dot(dir_coef.T, basis_rows, precision=highest).reshape(grid_shape)
        if sweep + 1 < ITERS:
            mode_image = apply_hessian(current, bond_vecs, bond_soft, onsite)
            search_image = apply_hessian(search, bond_vecs, bond_soft, onsite)
            image_image = apply_hessian(mode_image, bond_vecs, bond_soft, onsite)
    return (current, lowest)
```

```python
import functools
import math

import numpy as np
import jax
import jax.numpy as jnp
from jax import lax
from jax.experimental import pallas as pl
from jax.experimental.pallas import tpu as pltpu
from jax.sharding import PartitionSpec as P

ITERS = 2
MESH = pl.DeviceIdType.MESH
highest = lax.Precision.HIGHEST
offsets = ((1, 0), (0, 1), (1, 1), (1, -1), (-1, 0), (0, -1), (-1, -1), (-1, 1))

CUR, SRCH, IMG, IIMG, SIMG, THIRD, SIIMG = (32 * i for i in range(7))


def lowest_root_poly():
    nodes = np.cos(np.pi * (np.arange(64) + 0.5) / 64)
    level = 0.5 * (nodes + 1.0)
    root = np.cos(2.0 * np.arcsin(level) / 3.0 + 2.0 * np.pi / 3.0)
    cheb = np.polynomial.chebyshev.chebfit(nodes, root, 11)
    return [float(c) for c in np.polynomial.chebyshev.cheb2poly(cheb)]


ROOT_POLY = lowest_root_poly()


def lanes(rows=8):
    return lax.broadcasted_iota(jnp.int32, (rows, 128), 1)


def pencil_lowest(g, h):
    f = [[None] * 3 for _ in range(3)]
    inv = [[None] * 3 for _ in range(3)]
    recip = [None] * 3
    for i in range(3):
        for j in range(i + 1):
            pivot = g[i][j]
            for k in range(j):
                pivot = pivot - f[i][k] * f[j][k]
            if i == j:
                f[i][i] = jnp.sqrt(pivot)
                recip[i] = 1.0 / f[i][i]
            else:
                f[i][j] = pivot * recip[j]
    for j in range(3):
        inv[j][j] = recip[j]
        for i in range(j + 1, 3):
            acc = f[i][j] * inv[j][j]
            for k in range(j + 1, i):
                acc = acc + f[i][k] * inv[k][j]
            inv[i][j] = -acc * recip[i]
    half = [[sum(inv[i][j] * h[j][k] for j in range(i + 1)) for k in range(3)] for i in range(3)]
    b = [[None] * 3 for _ in range(3)]
    for i in range(3):
        for l in range(i + 1):
            b[i][l] = b[l][i] = sum(half[i][k] * inv[l][k] for k in range(l + 1))
    middle = (b[0][0] + b[1][1] + b[2][2]) * (1.0 / 3.0)
    c00, c11, c22 = b[0][0] - middle, b[1][1] - middle, b[2][2] - middle
    c01, c02, c12 = b[0][1], b[0][2], b[1][2]
    total = c00 * c00 + c11 * c11 + c22 * c22 + 2.0 * (c01 * c01 + c02 * c02 + c12 * c12)
    spread = jnp.sqrt(total * (1.0 / 6.0))
    det = (
        c00 * (c11 * c22 - c12 * c12)
        - c01 * (c01 * c22 - c12 * c02)
        + c02 * (c01 * c12 - c11 * c02)
    )
    cosine = jnp.clip(det / (2.0 * spread * spread * spread), -1.0, 1.0)
    u = 2.0 * jnp.sqrt((1.0 - cosine) * 0.5) - 1.0
    t = jnp.full_like(u, ROOT_POLY[-1])
    for coef in ROOT_POLY[-2::-1]:
        t = t * u + coef
    lowest = middle + 2.0 * spread * t
    p = [[h[i][j] - lowest * g[i][j] for j in range(3)] for i in range(3)]
    vector = (
        p[1][1] * p[2][2] - p[1][2] * p[2][1],
        p[1][2] * p[2][0] - p[1][0] * p[2][2],
        p[1][0] * p[2][1] - p[1][1] * p[2][0],
    )
    return lowest, vector


def inverse_factor(sym):
    lane, row = lanes(32), lax.broadcasted_iota(jnp.int32, (32, 128), 0)
    aug = jnp.where(lane < 32, (lane == row).astype(jnp.float32), pltpu.roll(sym, 32, 1))
    blocks = [aug[8 * b : 8 * b + 8] for b in range(4)]
    sub = lax.broadcasted_iota(jnp.int32, (8, 128), 0)
    for j in range(32):
        home, at = j // 8, j % 8
        pivot_row = blocks[home][at : at + 1]
        scaled = pivot_row * (1.0 / pivot_row[:, 32 + j : 33 + j])
        for b in range(home, 4):
            if b == home and at == 7:
                continue
            step = blocks[b][:, 32 + j : 33 + j] * scaled
            if b == home:
                step = jnp.where(sub > at, step, 0.0)
            blocks[b] = blocks[b] - step
    aug = jnp.concatenate(blocks, 0)
    pivots = jnp.sum(jnp.where(lane == row + 32, aug, 0.0), 1, keepdims=True)
    return jnp.where(lane < 32, aug / jnp.sqrt(pivots), 0.0)


def small_step(top, low):
    lane, row = lanes(32), lax.broadcasted_iota(jnp.int32, (32, 128), 0)
    beside = lane == 96 + (row + 1) % 32

    def diag(x, off):
        return jnp.sum(jnp.where(lane == row + off, x, 0.0), 1, keepdims=True)

    cc, cp, ca, ab = (diag(top, 32 * i) for i in range(4))
    aa, pp, pa, pb = (diag(low, 32 * i) for i in range(4))
    pq = jnp.sum(jnp.where(beside, low, 0.0), 1, keepdims=True)
    g = [[cc, ca, cp], [ca, aa, pa], [cp, pa, pp]]
    h = [[ca, aa, pa], [aa, ab, pb], [pa, pb, pq]]
    lowest, (v0, v1, v2) = pencil_lowest(g, h)
    dir_sq = v1 * v1 * aa + 2.0 * (v1 * v2) * pa + v2 * v2 * pp
    dir_scale = 1.0 / jnp.sqrt(dir_sq + 1e-06)

    def across(a, b, c, d):
        pick = jnp.where(lane < 64, jnp.where(lane < 32, a, b), jnp.where(lane < 96, c, d))
        return jnp.sum(jnp.where(lane % 32 == row, pick, 0.0), 0, keepdims=True)

    zero = jnp.zeros_like(v0)
    part = top * v0 * across(0.5 * v0, v2, v1, zero)
    part = part + low * jnp.where(lane < 32, v1, v2) * across(0.5 * v1, 0.5 * v2, v1, zero)
    folded = part + pltpu.roll(part, 96, 1) + pltpu.roll(part, 64, 1)
    folded = jnp.where(lane < 32, folded, 0.0)
    square = jnp.concatenate([folded, jnp.zeros((96, 128), jnp.float32)], 0)
    sym = folded + square.T[:32]
    linv = inverse_factor(sym)
    four = linv + pltpu.roll(linv, 32, 1) + pltpu.roll(linv, 64, 1) + pltpu.roll(linv, 96, 1)
    mixes = (
        four * across(v0, v2, v1, zero),
        four * across(v0, v1, v2, zero),
        four * across(v0, zero, v1, v2),
    )
    low_row = jnp.sum(jnp.where(lane == row, lowest, 0.0), 0, keepdims=True)
    return low_row, mixes, v1 * dir_scale, v2 * dir_scale


def kernel(
    nx,
    ny,
    entries,
    modes_ref,
    dirs_ref,
    onsite_ref,
    bond_ref,
    contact_ref,
    out_ref,
    low_ref,
    basis,
    basis2,
    coef,
    pack,
    col_in,
    diag_in,
    row_in,
    slots_y,
    slots_x,
    halo_send,
    halo_recv,
    y_send,
    y_recv,
    x_send,
    x_recv,
):
    part, gx, gy = lax.axis_index("pack"), lax.axis_index("gx"), lax.axis_index("gy")

    def peer(dx, dy):
        return (part, lax.rem(gx + dx + nx, nx), lax.rem(gy + dy + ny, ny))

    diagonals = ((-1, -1), (-1, 1), (1, -1), (1, 1))
    peers = [peer(0, o) for o in range(1, ny)] + [peer(o, 0) for o in range(1, nx)]
    peers += [peer(*d) for d in diagonals]
    barrier = pltpu.get_barrier_semaphore()
    for device in peers:
        pl.semaphore_signal(barrier, inc=1, device_id=device, device_id_type=MESH)

    lane8 = lanes(8)

    def eight(block, base=0):
        return pl.ds(pl.multiple_of(base + 8 * block, 8), 8)

    for x in range(8):
        for c in range(3):
            basis[3 * x + c, CUR : CUR + 32] = modes_ref[pl.ds(8 * c + x, 32, stride=24), :]
            basis[3 * x + c, SRCH : SRCH + 32] = dirs_ref[pl.ds(8 * c + x, 32, stride=24), :]
    for d in range(8):
        on = contact_ref[d].astype(jnp.float32)
        for t in range(4):
            coef[4 * d + t] = bond_ref[d, t] * on
    for c in range(3):
        coef[32 + c] = onsite_ref[c]

    def pack_edges(e, fields):
        def block(b, carry):
            first = jnp.zeros((8, 128), jnp.float32)
            last = jnp.zeros((8, 128), jnp.float32)
            for f, base in enumerate(fields):
                for q in range(24):
                    lane = 32 * f + q
                    u = basis[q, eight(b, base), :]
                    at_lane = lane8 == lane
                    first = jnp.where(at_lane, pltpu.roll(u, lane, 1) if lane else u, first)
                    last = jnp.where(at_lane, pltpu.roll(u, lane + 1, 1), last)
            pack[e, 0, eight(b), :] = first
            pack[e, 1, eight(b), :] = last
            return carry

        lax.fori_loop(0, 4, block, 0)

    def halo_copies(e, base, height):
        plan = []
        rows = pl.ds(base, height)
        plan.append((basis.at[pl.ds(21, 3), rows], row_in.at[e, 0, :, pl.ds(0, height)], (1, 0)))
        plan.append((basis.at[pl.ds(0, 3), rows], row_in.at[e, 1, :, pl.ds(0, height)], (-1, 0)))
        plan.append((pack.at[e, 1], col_in.at[e, 0], (0, 1)))
        plan.append((pack.at[e, 0], col_in.at[e, 1], (0, -1)))
        for k, (sx, sy) in enumerate(diagonals):
            plan.append((pack.at[e, 1 if sy < 0 else 0], diag_in.at[e, k], (-sx, -sy)))
        return [
            pltpu.make_async_remote_copy(
                src_ref=src,
                dst_ref=dst,
                send_sem=halo_send.at[e, k],
                recv_sem=halo_recv.at[e, k],
                device_id=peer(*to),
                device_id_type=MESH,
            )
            for k, (src, dst, to) in enumerate(plan)
        ]

    def apply(e, f, base, out_base):
        def block(b, carry):
            left, right = col_in[e, 0, eight(b), :], col_in[e, 1, eight(b), :]
            corners = [diag_in[e, k, eight(b), :] for k in range(4)]

            def three(x, c):
                if x < 0:
                    u = row_in[e, 0, c, eight(b, 32 * f), :]
                    lane, before, after = 32 * f + 21 + c, corners[0], corners[1]
                elif x > 7:
                    u = row_in[e, 1, c, eight(b, 32 * f), :]
                    lane, before, after = 32 * f + c, corners[2], corners[3]
                else:
                    u = basis[3 * x + c, eight(b, base), :]
                    lane, before, after = 32 * f + 3 * x + c, left, right
                before = pltpu.roll(before, 128 - lane, 1) if lane else before
                after = pltpu.roll(after, 127 - lane, 1)
                return {
                    0: u,
                    -1: jnp.where(lane8 == 0, before, pltpu.roll(u, 1, 1)),
                    1: jnp.where(lane8 == 127, after, pltpu.roll(u, 127, 1)),
                }

            window = {x: [three(x, c) for c in range(3)] for x in (-1, 0)}
            for x in range(8):
                window[x + 1] = [three(x + 1, c) for c in range(3)]
                field = [window[x][c][0] for c in range(3)]
                result = [coef[32 + c, x : x + 1, :] * field[c] for c in range(3)]
                for d, (dx, dy) in enumerate(offsets):
                    a = [coef[4 * d + c, x : x + 1, :] for c in range(3)]
                    soft = coef[4 * d + 3, x : x + 1, :]
                    stretch = [field[c] - window[x + dx][c][dy] for c in range(3)]
                    along = a[0] * stretch[0] + a[1] * stretch[1] + a[2] * stretch[2]
                    result = [result[c] + (a[c] * along + soft * stretch[c]) for c in range(3)]
                for c in range(3):
                    basis[3 * x + c, eight(b, out_base), :] = result[c]
            return carry

        lax.fori_loop(0, 4, block, 0)

    lane32, row32 = lanes(32), lax.broadcasted_iota(jnp.int32, (32, 128), 0)

    def local_sums(ref):
        total = jnp.zeros((96, 128), jnp.float32)
        cross = jnp.zeros((32, 128), jnp.float32)
        for q in range(0, 24, 2):
            rows = jnp.concatenate([ref[q, 0:128, :], ref[q + 1, 0:128, :]], 1)
            total = total + lax.dot_general(
                rows[:96],
                rows,
                (((1,), (1,)), ((), ())),
                precision=highest,
                preferred_element_type=jnp.float32,
            )
            for i in (q, q + 1):
                cross = cross + ref[i, SRCH : SRCH + 32, :] * ref[i, SIMG : SIMG + 32, :]
        cross = jnp.sum(cross, 1, keepdims=True)
        img_rows = total[64:96]
        top = jnp.where(lane32 < 96, total[0:32], img_rows)
        low = jnp.where(lane32 < 32, pltpu.roll(img_rows, 64, 1), total[32:64])
        low = jnp.where(lane32 == 96 + (row32 + 1) % 32, cross, low)
        return jnp.concatenate([top, low], 0)

    def sum_start(slots, n, me, axis, sweep, send, recv, value):
        slots[sweep, me] = value
        copies = []
        for o in range(1, n):
            copy = pltpu.make_async_remote_copy(
                src_ref=slots.at[sweep, me],
                dst_ref=slots.at[sweep, me],
                send_sem=send.at[sweep, o - 1],
                recv_sem=recv.at[sweep, o - 1],
                device_id=peer(o, 0) if axis == "x" else peer(0, o),
                device_id_type=MESH,
            )
            copy.start()
            copies.append(copy)
        return copies

    def sum_finish(slots, n, sweep, copies):
        for copy in copies:
            copy.wait_recv()
        total = slots[sweep, 0]
        for i in range(1, n):
            total = total + slots[sweep, i]
        return total

    sent = []

    def exchange(e, base, height):
        copies = halo_copies(e, base, height)
        for copy in copies:
            copy.start()
        sent.extend(copies)
        return copies

    pack_edges(0, (CUR, SRCH))
    pl.semaphore_wait(barrier, len(peers))
    first = exchange(0, CUR, 64)
    for copy in first:
        copy.wait_recv()
    apply(0, 0, CUR, IMG)
    pack_edges(1, (IMG,))
    second = exchange(1, IMG, 32)
    apply(0, 1, SRCH, SIMG)
    for copy in second:
        copy.wait_recv()
    apply(1, 0, IMG, IIMG)

    along_y = sum_start(slots_y, ny, gy, "y", 0, y_send, y_recv, local_sums(basis))
    sent.extend(along_y)
    pack_edges(2, (IIMG, SIMG))
    third = exchange(2, IIMG, 64)
    value = sum_finish(slots_y, ny, 0, along_y)
    along_x = sum_start(slots_x, nx, gx, "x", 0, x_send, x_recv, value)
    sent.extend(along_x)
    for copy in third:
        copy.wait_recv()
    apply(2, 0, IIMG, THIRD)
    apply(2, 1, SIMG, SIIMG)
    sums = sum_finish(slots_x, nx, 0, along_x) * (1.0 / entries)
    _, mixes, on_img, on_srch = small_step(sums[:32], sums[32:])

    def mixed(mix, ref, q, base):
        return jnp.dot(
            mix,
            jnp.concatenate([ref[q, base : base + 128, :], ref[q + 1, base : base + 128, :]], 1),
            precision=highest,
            preferred_element_type=jnp.float32,
        )

    for q in range(0, 24, 2):
        for mix, base, into in zip(mixes, (CUR, IMG, IIMG), (CUR, IMG, IIMG)):
            value = mixed(mix, basis, q, base)
            basis2[q, into : into + 32, :] = value[:, :128]
            basis2[q + 1, into : into + 32, :] = value[:, 128:]
        for i in (q, q + 1):
            for old_img, old, into in ((IMG, SRCH, SRCH), (IIMG, SIMG, SIMG)):
                basis2[i, into : into + 32, :] = (
                    on_img * basis[i, old_img : old_img + 32, :]
                    + on_srch * basis[i, old : old + 32, :]
                )

    along_y = sum_start(slots_y, ny, gy, "y", 1, y_send, y_recv, local_sums(basis2))
    sent.extend(along_y)
    value = sum_finish(slots_y, ny, 1, along_y)
    along_x = sum_start(slots_x, nx, gx, "x", 1, x_send, x_recv, value)
    sent.extend(along_x)
    sums = sum_finish(slots_x, nx, 1, along_x) * (1.0 / entries)
    lowest, mixes, _, _ = small_step(sums[:32], sums[32:])
    low_ref[...] = lowest
    for q in range(0, 24, 2):
        value = mixed(mixes[0], basis2, q, CUR)
        for i in (q, q + 1):
            x, c = i // 3, i % 3
            out_ref[pl.ds(8 * c + x, 32, stride=24), :] = value[:, 128 * (i - q) : 128 * (i - q) + 128]
    for copy in sent:
        copy.wait_send()


def solution(mesh):
    nx, ny = mesh.shape["gx"], mesh.shape["gy"]

    def body(modes_in, dirs_in, onsite, bond_terms, contacts):
        shape = modes_in.shape
        entries = float(3 * shape[2] * shape[3] * nx * ny)
        vmem = pl.BlockSpec(memory_space=pltpu.VMEM)
        f32 = jnp.float32
        modes, lowest = pl.pallas_call(
            functools.partial(kernel, nx, ny, entries),
            out_shape=(
                jax.ShapeDtypeStruct((768, 128), f32),
                jax.ShapeDtypeStruct((1, 128), f32),
            ),
            in_specs=[vmem] * 5,
            out_specs=(vmem, vmem),
            scratch_shapes=[
                pltpu.VMEM((24, 224, 128), f32),
                pltpu.VMEM((24, 160, 128), f32),
                pltpu.VMEM((35, 8, 128), f32),
                pltpu.VMEM((3, 2, 32, 128), f32),
                pltpu.VMEM((3, 2, 32, 128), f32),
                pltpu.VMEM((3, 4, 32, 128), f32),
                pltpu.VMEM((3, 2, 3, 64, 128), f32),
                pltpu.VMEM((2, ny, 64, 128), f32),
                pltpu.VMEM((2, nx, 64, 128), f32),
                pltpu.SemaphoreType.DMA((3, 8)),
                pltpu.SemaphoreType.DMA((3, 8)),
                pltpu.SemaphoreType.DMA((2, ny - 1)),
                pltpu.SemaphoreType.DMA((2, ny - 1)),
                pltpu.SemaphoreType.DMA((2, nx - 1)),
                pltpu.SemaphoreType.DMA((2, nx - 1)),
            ],
            compiler_params=pltpu.CompilerParams(
                collective_id=0, has_side_effects=True, vmem_limit_bytes=32 * 1024 * 1024
            ),
        )(
            modes_in.reshape(768, 128),
            dirs_in.reshape(768, 128),
            onsite,
            bond_terms,
            contacts,
        )
        return modes.reshape(shape), lowest[0, : shape[0]]

    in_specs = (
        P(None, None, ("pack", "gx"), "gy"),
        P(None, None, ("pack", "gx"), "gy"),
        P(None, ("pack", "gx"), "gy"),
        P(None, None, ("pack", "gx"), "gy"),
        P(None, ("pack", "gx"), "gy"),
    )
    out_specs = (P(None, None, ("pack", "gx"), "gy"), P("pack"))
    return jax.shard_map(body, mesh=mesh, in_specs=in_specs, out_specs=out_specs, check_vma=False)
```

```python
import functools
import math

import numpy as np
import jax
import jax.numpy as jnp
from jax import lax
from jax.experimental import pallas as pl
from jax.experimental.pallas import tpu as pltpu
from jax.sharding import PartitionSpec as P

ITERS = 2
MESH = pl.DeviceIdType.MESH
highest = lax.Precision.HIGHEST
offsets = ((1, 0), (0, 1), (1, 1), (1, -1), (-1, 0), (0, -1), (-1, -1), (-1, 1))

CUR, SRCH, IMG, IIMG, SIMG, THIRD, SIIMG = (32 * i for i in range(7))


def lowest_root_poly():
    nodes = np.cos(np.pi * (np.arange(64) + 0.5) / 64)
    level = 0.5 * (nodes + 1.0)
    root = np.cos(2.0 * np.arcsin(level) / 3.0 + 2.0 * np.pi / 3.0)
    cheb = np.polynomial.chebyshev.chebfit(nodes, root, 11)
    return [float(c) for c in np.polynomial.chebyshev.cheb2poly(cheb)]


ROOT_POLY = lowest_root_poly()


def lanes(rows=8):
    return lax.broadcasted_iota(jnp.int32, (rows, 128), 1)


def pencil_lowest(g, h):
    f = [[None] * 3 for _ in range(3)]
    inv = [[None] * 3 for _ in range(3)]
    recip = [None] * 3
    for i in range(3):
        for j in range(i + 1):
            pivot = g[i][j]
            for k in range(j):
                pivot = pivot - f[i][k] * f[j][k]
            if i == j:
                f[i][i] = jnp.sqrt(pivot)
                recip[i] = 1.0 / f[i][i]
            else:
                f[i][j] = pivot * recip[j]
    for j in range(3):
        inv[j][j] = recip[j]
        for i in range(j + 1, 3):
            acc = f[i][j] * inv[j][j]
            for k in range(j + 1, i):
                acc = acc + f[i][k] * inv[k][j]
            inv[i][j] = -acc * recip[i]
    half = [[sum(inv[i][j] * h[j][k] for j in range(i + 1)) for k in range(3)] for i in range(3)]
    b = [[None] * 3 for _ in range(3)]
    for i in range(3):
        for l in range(i + 1):
            b[i][l] = b[l][i] = sum(half[i][k] * inv[l][k] for k in range(l + 1))
    middle = (b[0][0] + b[1][1] + b[2][2]) * (1.0 / 3.0)
    c00, c11, c22 = b[0][0] - middle, b[1][1] - middle, b[2][2] - middle
    c01, c02, c12 = b[0][1], b[0][2], b[1][2]
    total = c00 * c00 + c11 * c11 + c22 * c22 + 2.0 * (c01 * c01 + c02 * c02 + c12 * c12)
    spread = jnp.sqrt(total * (1.0 / 6.0))
    det = (
        c00 * (c11 * c22 - c12 * c12)
        - c01 * (c01 * c22 - c12 * c02)
        + c02 * (c01 * c12 - c11 * c02)
    )
    cosine = jnp.clip(det / (2.0 * spread * spread * spread), -1.0, 1.0)
    u = 2.0 * jnp.sqrt((1.0 - cosine) * 0.5) - 1.0
    t = jnp.full_like(u, ROOT_POLY[-1])
    for coef in ROOT_POLY[-2::-1]:
        t = t * u + coef
    lowest = middle + 2.0 * spread * t
    p = [[h[i][j] - lowest * g[i][j] for j in range(3)] for i in range(3)]
    vector = (
        p[1][1] * p[2][2] - p[1][2] * p[2][1],
        p[1][2] * p[2][0] - p[1][0] * p[2][2],
        p[1][0] * p[2][1] - p[1][1] * p[2][0],
    )
    return lowest, vector


def inverse_factor(sym):
    lane, row = lanes(32), lax.broadcasted_iota(jnp.int32, (32, 128), 0)
    aug = jnp.where(lane < 32, (lane == row).astype(jnp.float32), pltpu.roll(sym, 32, 1))
    blocks = [aug[8 * b : 8 * b + 8] for b in range(4)]
    sub = lax.broadcasted_iota(jnp.int32, (8, 128), 0)
    for home in range(4):
        cols = {
            b: [
                jnp.broadcast_to(blocks[b][:, 32 + 8 * home + i : 33 + 8 * home + i], (8, 128))
                for i in range(8)
            ]
            for b in range(home, 4)
        }
        for i in range(8):
            recip = 1.0 / cols[home][i][i : i + 1]
            scaled = blocks[home][i : i + 1] * recip
            ratios = {k: cols[home][k][i : i + 1] * recip for k in range(i + 1, 8)}
            for b in range(home, 4):
                factor = jnp.where(sub > i, cols[b][i], 0.0) if b == home else cols[b][i]
                blocks[b] = blocks[b] - factor * scaled
                for k, ratio in ratios.items():
                    cols[b][k] = cols[b][k] - factor * ratio
    aug = jnp.concatenate(blocks, 0)
    pivots = jnp.sum(jnp.where(lane == row + 32, aug, 0.0), 1, keepdims=True)
    return jnp.where(lane < 32, aug / jnp.sqrt(pivots), 0.0)


def small_step(top, low):
    lane, row = lanes(32), lax.broadcasted_iota(jnp.int32, (32, 128), 0)
    beside = lane == 96 + (row + 1) % 32

    def diag(x, off):
        return jnp.sum(jnp.where(lane == row + off, x, 0.0), 1, keepdims=True)

    cc, cp, ca, ab = (diag(top, 32 * i) for i in range(4))
    aa, pp, pa, pb = (diag(low, 32 * i) for i in range(4))
    pq = jnp.sum(jnp.where(beside, low, 0.0), 1, keepdims=True)
    g = [[cc, ca, cp], [ca, aa, pa], [cp, pa, pp]]
    h = [[ca, aa, pa], [aa, ab, pb], [pa, pb, pq]]
    lowest, (v0, v1, v2) = pencil_lowest(g, h)
    dir_sq = v1 * v1 * aa + 2.0 * (v1 * v2) * pa + v2 * v2 * pp
    dir_scale = 1.0 / jnp.sqrt(dir_sq + 1e-06)

    def across(a, b, c, d):
        pick = jnp.where(lane < 64, jnp.where(lane < 32, a, b), jnp.where(lane < 96, c, d))
        return jnp.sum(jnp.where(lane % 32 == row, pick, 0.0), 0, keepdims=True)

    zero = jnp.zeros_like(v0)
    part = top * v0 * across(0.5 * v0, v2, v1, zero)
    part = part + low * jnp.where(lane < 32, v1, v2) * across(0.5 * v1, 0.5 * v2, v1, zero)
    folded = part + pltpu.roll(part, 96, 1) + pltpu.roll(part, 64, 1)
    folded = jnp.where(lane < 32, folded, 0.0)
    square = jnp.concatenate([folded, jnp.zeros((96, 128), jnp.float32)], 0)
    sym = folded + square.T[:32]
    linv = inverse_factor(sym)
    four = linv + pltpu.roll(linv, 32, 1) + pltpu.roll(linv, 64, 1) + pltpu.roll(linv, 96, 1)
    mixes = (
        four * across(v0, v2, v1, zero),
        four * across(v0, v1, v2, zero),
        four * across(v0, zero, v1, v2),
    )
    low_row = jnp.sum(jnp.where(lane == row, lowest, 0.0), 0, keepdims=True)
    return low_row, mixes, v1 * dir_scale, v2 * dir_scale


def kernel(
    nx,
    ny,
    entries,
    modes_hbm,
    dirs_hbm,
    onsite_hbm,
    bond_hbm,
    contact_hbm,
    out_ref,
    low_ref,
    modes_ref,
    dirs_ref,
    onsite_ref,
    bond_ref,
    contact_ref,
    load_sem,
    basis,
    basis2,
    coef,
    pack,
    col_in,
    diag_in,
    row_in,
    slots_y,
    slots_x,
    halo_send,
    halo_recv,
    y_send,
    y_recv,
    x_send,
    x_recv,
):
    held = (
        (modes_hbm, modes_ref),
        (dirs_hbm, dirs_ref),
        (bond_hbm, bond_ref),
        (contact_hbm, contact_ref),
        (onsite_hbm, onsite_ref),
    )
    loads = [pltpu.make_async_copy(a, b, load_sem.at[i]) for i, (a, b) in enumerate(held)]
    for load in loads:
        load.start()
    part, gx, gy = lax.axis_index("pack"), lax.axis_index("gx"), lax.axis_index("gy")

    def peer(dx, dy):
        return (part, lax.rem(gx + dx + nx, nx), lax.rem(gy + dy + ny, ny))

    diagonals = ((-1, -1), (-1, 1), (1, -1), (1, 1))
    peers = [peer(0, o) for o in range(1, ny)] + [peer(o, 0) for o in range(1, nx)]
    peers += [peer(*d) for d in diagonals]
    barrier = pltpu.get_barrier_semaphore()
    for device in peers:
        pl.semaphore_signal(barrier, inc=1, device_id=device, device_id_type=MESH)

    lane8 = lanes(8)

    def eight(block, base=0):
        return pl.ds(pl.multiple_of(base + 8 * block, 8), 8)

    def take(load, base, ref):
        load.wait()
        for x in range(8):
            for c in range(3):
                basis[3 * x + c, base : base + 32] = ref[pl.ds(8 * c + x, 32, stride=24), :]

    def pack_edges(e, base):
        first = jnp.zeros((8, 128), jnp.float32)
        last = jnp.zeros((8, 128), jnp.float32)
        for b in range(4):
            for q in range(24):
                lane = 32 * b + q
                u = basis[q, base + 8 * b : base + 8 * b + 8, :]
                at_lane = lane8 == lane
                first = jnp.where(at_lane, pltpu.roll(u, lane, 1) if lane else u, first)
                last = jnp.where(at_lane, pltpu.roll(u, lane + 1, 1), last)
        pack[e, 0] = first
        pack[e, 1] = last

    def halo_copies(e, base):
        plan = []
        rows = pl.ds(base, 32)
        plan.append((basis.at[pl.ds(21, 3), rows], row_in.at[e, 0], (1, 0)))
        plan.append((basis.at[pl.ds(0, 3), rows], row_in.at[e, 1], (-1, 0)))
        plan.append((pack.at[e, 1], col_in.at[e, 0], (0, 1)))
        plan.append((pack.at[e, 0], col_in.at[e, 1], (0, -1)))
        for k, (sx, sy) in enumerate(diagonals):
            plan.append((pack.at[e, 1 if sy < 0 else 0], diag_in.at[e, k], (-sx, -sy)))
        return [
            pltpu.make_async_remote_copy(
                src_ref=src,
                dst_ref=dst,
                send_sem=halo_send.at[e, k],
                recv_sem=halo_recv.at[e, k],
                device_id=peer(*to),
                device_id_type=MESH,
            )
            for k, (src, dst, to) in enumerate(plan)
        ]

    def apply(e, base, out_base):
        def block(b, carry):
            shift = lax.rem(96 * b, 128)
            left, right = (pltpu.roll(col_in[e, k], shift, 1) for k in range(2))
            corners = [pltpu.roll(diag_in[e, k], shift, 1) for k in range(4)]

            def three(x, c):
                if x < 0:
                    u = row_in[e, 0, c, eight(b), :]
                    lane, before, after = 21 + c, corners[0], corners[1]
                elif x > 7:
                    u = row_in[e, 1, c, eight(b), :]
                    lane, before, after = c, corners[2], corners[3]
                else:
                    u = basis[3 * x + c, eight(b, base), :]
                    lane, before, after = 3 * x + c, left, right
                before = pltpu.roll(before, 128 - lane, 1) if lane else before
                after = pltpu.roll(after, 127 - lane, 1)
                return {
                    0: u,
                    -1: jnp.where(lane8 == 0, before, pltpu.roll(u, 1, 1)),
                    1: jnp.where(lane8 == 127, after, pltpu.roll(u, 127, 1)),
                }

            window = {x: [three(x, c) for c in range(3)] for x in (-1, 0)}
            for x in range(8):
                window[x + 1] = [three(x + 1, c) for c in range(3)]
                field = [window[x][c][0] for c in range(3)]
                result = [coef[32 + c, x : x + 1, :] * field[c] for c in range(3)]
                for d, (dx, dy) in enumerate(offsets):
                    a = [coef[4 * d + c, x : x + 1, :] for c in range(3)]
                    soft = coef[4 * d + 3, x : x + 1, :]
                    stretch = [field[c] - window[x + dx][c][dy] for c in range(3)]
                    along = a[0] * stretch[0] + a[1] * stretch[1] + a[2] * stretch[2]
                    result = [result[c] + (a[c] * along + soft * stretch[c]) for c in range(3)]
                for c in range(3):
                    basis[3 * x + c, eight(b, out_base), :] = result[c]
            return carry

        lax.fori_loop(0, 4, block, 0)

    lane32, row32 = lanes(32), lax.broadcasted_iota(jnp.int32, (32, 128), 0)

    def local_sums(ref):
        total = jnp.zeros((96, 128), jnp.float32)
        cross = jnp.zeros((32, 128), jnp.float32)
        for q in range(0, 24, 2):
            rows = jnp.concatenate([ref[q, 0:128, :], ref[q + 1, 0:128, :]], 1)
            total = total + lax.dot_general(
                rows[:96],
                rows,
                (((1,), (1,)), ((), ())),
                precision=highest,
                preferred_element_type=jnp.float32,
            )
            for i in (q, q + 1):
                cross = cross + ref[i, SRCH : SRCH + 32, :] * ref[i, SIMG : SIMG + 32, :]
        cross = jnp.sum(cross, 1, keepdims=True)
        img_rows = total[64:96]
        top = jnp.where(lane32 < 96, total[0:32], img_rows)
        low = jnp.where(lane32 < 32, pltpu.roll(img_rows, 64, 1), total[32:64])
        low = jnp.where(lane32 == 96 + (row32 + 1) % 32, cross, low)
        return jnp.concatenate([top, low], 0)

    def sum_start(slots, n, me, axis, sweep, send, recv, value):
        slots[sweep, me] = value
        copies = []
        for o in range(1, n):
            copy = pltpu.make_async_remote_copy(
                src_ref=slots.at[sweep, me],
                dst_ref=slots.at[sweep, me],
                send_sem=send.at[sweep, o - 1],
                recv_sem=recv.at[sweep, o - 1],
                device_id=peer(o, 0) if axis == "x" else peer(0, o),
                device_id_type=MESH,
            )
            copy.start()
            copies.append(copy)
        return copies

    def sum_finish(slots, n, sweep, copies):
        for copy in copies:
            copy.wait_recv()
        total = slots[sweep, 0]
        for i in range(1, n):
            total = total + slots[sweep, i]
        return total

    sent = []

    def exchange(e, base):
        copies = halo_copies(e, base)
        for copy in copies:
            copy.start()
        sent.extend(copies)
        return copies

    def arrived(copies):
        for copy in copies:
            copy.wait_recv()

    take(loads[0], CUR, modes_ref)
    pack_edges(0, CUR)
    pl.semaphore_wait(barrier, len(peers))
    of_cur = exchange(0, CUR)
    take(loads[1], SRCH, dirs_ref)
    pack_edges(1, SRCH)
    of_srch = exchange(1, SRCH)
    for load in loads[2:]:
        load.wait()
    for d in range(8):
        on = contact_ref[d].astype(jnp.float32)
        for t in range(4):
            coef[4 * d + t] = bond_ref[d, t] * on
    for c in range(3):
        coef[32 + c] = onsite_ref[c]
    arrived(of_cur)
    apply(0, CUR, IMG)
    pack_edges(2, IMG)
    of_img = exchange(2, IMG)
    arrived(of_srch)
    apply(1, SRCH, SIMG)
    pack_edges(3, SIMG)
    arrived(of_img)
    of_simg = exchange(3, SIMG)
    apply(2, IMG, IIMG)

    along_y = sum_start(slots_y, ny, gy, "y", 0, y_send, y_recv, local_sums(basis))
    sent.extend(along_y)
    pack_edges(4, IIMG)
    of_iimg = exchange(4, IIMG)
    value = sum_finish(slots_y, ny, 0, along_y)
    along_x = sum_start(slots_x, nx, gx, "x", 0, x_send, x_recv, value)
    sent.extend(along_x)
    arrived(of_simg)
    apply(3, SIMG, SIIMG)
    arrived(of_iimg)
    apply(4, IIMG, THIRD)
    sums = sum_finish(slots_x, nx, 0, along_x) * (1.0 / entries)
    _, mixes, on_img, on_srch = small_step(sums[:32], sums[32:])

    def mixed(mix, ref, q, base):
        return jnp.dot(
            mix,
            jnp.concatenate([ref[q, base : base + 128, :], ref[q + 1, base : base + 128, :]], 1),
            precision=highest,
            preferred_element_type=jnp.float32,
        )

    for q in range(0, 24, 2):
        for mix, base, into in zip(mixes, (CUR, IMG, IIMG), (CUR, IMG, IIMG)):
            value = mixed(mix, basis, q, base)
            basis2[q, into : into + 32, :] = value[:, :128]
            basis2[q + 1, into : into + 32, :] = value[:, 128:]
        for i in (q, q + 1):
            for old_img, old, into in ((IMG, SRCH, SRCH), (IIMG, SIMG, SIMG)):
                basis2[i, into : into + 32, :] = (
                    on_img * basis[i, old_img : old_img + 32, :]
                    + on_srch * basis[i, old : old + 32, :]
                )

    along_y = sum_start(slots_y, ny, gy, "y", 1, y_send, y_recv, local_sums(basis2))
    sent.extend(along_y)
    value = sum_finish(slots_y, ny, 1, along_y)
    along_x = sum_start(slots_x, nx, gx, "x", 1, x_send, x_recv, value)
    sent.extend(along_x)
    sums = sum_finish(slots_x, nx, 1, along_x) * (1.0 / entries)
    lowest, mixes, _, _ = small_step(sums[:32], sums[32:])
    low_ref[...] = lowest
    for q in range(0, 24, 2):
        value = mixed(mixes[0], basis2, q, CUR)
        for i in (q, q + 1):
            x, c = i // 3, i % 3
            out_ref[pl.ds(8 * c + x, 32, stride=24), :] = value[:, 128 * (i - q) : 128 * (i - q) + 128]
    for copy in sent:
        copy.wait_send()


def solution(mesh):
    nx, ny = mesh.shape["gx"], mesh.shape["gy"]

    def body(modes_in, dirs_in, onsite, bond_terms, contacts):
        shape = modes_in.shape
        entries = float(3 * shape[2] * shape[3] * nx * ny)
        vmem = pl.BlockSpec(memory_space=pltpu.VMEM)
        f32 = jnp.float32
        modes, lowest = pl.pallas_call(
            functools.partial(kernel, nx, ny, entries),
            out_shape=(
                jax.ShapeDtypeStruct((768, 128), f32),
                jax.ShapeDtypeStruct((1, 128), f32),
            ),
            in_specs=[pl.BlockSpec(memory_space=pltpu.HBM)] * 5,
            out_specs=(vmem, vmem),
            scratch_shapes=[
                pltpu.VMEM((768, 128), f32),
                pltpu.VMEM((768, 128), f32),
                pltpu.VMEM(onsite.shape, f32),
                pltpu.VMEM(bond_terms.shape, f32),
                pltpu.VMEM(contacts.shape, jnp.int32),
                pltpu.SemaphoreType.DMA((5,)),
                pltpu.VMEM((24, 224, 128), f32),
                pltpu.VMEM((24, 160, 128), f32),
                pltpu.VMEM((35, 8, 128), f32),
                pltpu.VMEM((5, 2, 8, 128), f32),
                pltpu.VMEM((5, 2, 8, 128), f32),
                pltpu.VMEM((5, 4, 8, 128), f32),
                pltpu.VMEM((5, 2, 3, 32, 128), f32),
                pltpu.VMEM((2, ny, 64, 128), f32),
                pltpu.VMEM((2, nx, 64, 128), f32),
                pltpu.SemaphoreType.DMA((5, 8)),
                pltpu.SemaphoreType.DMA((5, 8)),
                pltpu.SemaphoreType.DMA((2, ny - 1)),
                pltpu.SemaphoreType.DMA((2, ny - 1)),
                pltpu.SemaphoreType.DMA((2, nx - 1)),
                pltpu.SemaphoreType.DMA((2, nx - 1)),
            ],
            compiler_params=pltpu.CompilerParams(
                collective_id=0, has_side_effects=True, vmem_limit_bytes=60 * 1024 * 1024
            ),
        )(
            modes_in.reshape(768, 128),
            dirs_in.reshape(768, 128),
            onsite,
            bond_terms,
            contacts,
        )
        return modes.reshape(shape), lowest[0, : shape[0]]

    in_specs = (
        P(None, None, ("pack", "gx"), "gy"),
        P(None, None, ("pack", "gx"), "gy"),
        P(None, ("pack", "gx"), "gy"),
        P(None, None, ("pack", "gx"), "gy"),
        P(None, ("pack", "gx"), "gy"),
    )
    out_specs = (P(None, None, ("pack", "gx"), "gy"), P("pack"))
    return jax.shard_map(body, mesh=mesh, in_specs=in_specs, out_specs=out_specs, check_vma=False)
```
